32 devices in a mesh: rep: 8 (over y, x, core), exp: 4 (over z).
Axes of the slice: x: 2, y: 2, z: 4, core: 2. Of those that a mesh axis runs over, the one named last changes fastest.
Arguments:
- hidden: bfloat16 [4096, 4096], P(('rep', 'exp')), may hold values from -6 to 6
- parents: int32 [4096], P(('rep', 'exp')), may hold values from 0 to 511
- routes: int32 [4096, 8], P(('rep', 'exp')), may hold values from 0 to 31, all different within a row; in each aligned block of 128 rows (0 to 127, 128 to 255, ...) at most 34 rows name the same one
- gates: float32 [4096, 8], P(('rep', 'exp')), may hold values from 0.05 to 1
- counts: int32 [32], P(('rep', 'exp')), may hold values from 64 to 128, as said below
- norm_gain: float32 [4096], replicated, may hold values from 0.1 to 1.9
- w_gate: bfloat16 [32, 4096, 768], P(('rep', 'exp')), may hold values from -0.09375 to 0.09375
- w_up: bfloat16 [32, 4096, 768], P(('rep', 'exp')), may hold values from -0.09375 to 0.09375
- w_down: bfloat16 [32, 768, 4096], P(('rep', 'exp')), may hold values from -0.21875 to 0.21875
Outputs:
- mixed: bfloat16 [4096, 4096], P(('rep', 'exp'))
The draws below stay inside these ranges and needn't reach their ends.
Inputs may be any that keep to these rules, and one draw needn't show every extreme that they name: `routes`: in the rows of one device no expert is named more than 34 times. `counts`: some device has all of its rows live.
All inputs are finite; a program needn't handle non-finite values.
Results may differ from the reference program's by a relative error of at most 0.0071.
Values may be sent and summed in bfloat16 or wider, within the bound.
No kernel may reach another device: no remote copies, remote signals or barrier semaphores. Data moves between devices by JAX's collectives and lax.ppermute only.
A program may use at most 128 MiB of HBM per device.

```python
import math
import jax
import jax.numpy as jnp
import numpy as np
from jax import lax

D = 4096
FFW = 768
TOP = 8
ROWS_DEV = 128
EXPERTS = 32
BLOCKS = 32
MICRO = 512
ROWS = 4096
CAP = 34
N_EXP = 4


def draw_counts(key, part):
    base = jax.random.randint(key, (BLOCKS,), ROWS_DEV // 2, ROWS_DEV + 1)
    chosen = jax.random.randint(jax.random.fold_in(key, 7), (), 0, BLOCKS)
    return jnp.where(jnp.arange(BLOCKS) == chosen, ROWS_DEV, base).astype(jnp.int32)


def place_ends(array, own_key, low, high):
    extent = array.shape
    index_at = [jax.random.randint(jax.random.fold_in(own_key, axis), (), 0, extent[axis]) for axis in range(len(extent))]
    array = array.at[tuple(index_at)].set(low)
    longest = extent.index(max(extent))
    index_at[longest] = (index_at[longest] + 1) % extent[longest]
    return array.at[tuple(index_at)].set(high)


def levels(stream_key, extent, split, least, largest):
    factor_of, own = 1.0, jax.random.fold_in(stream_key, 6)
    for dim, blocks in split:
        draws = jnp.exp(jax.random.uniform(jax.random.fold_in(own, dim), (blocks,), jnp.float32, least / len(split), largest / len(split)))
        factor_of = factor_of * jnp.repeat(draws, extent[dim] // blocks).reshape([-1 if axis == dim else 1 for axis in range(len(extent))])
    return factor_of


def shared_out(stream_key, own, number, rows, number_of, top, most, skew):
    sequence = jax.random.permutation(stream_key, number_of)
    packed, ordinary = load_shares(number_of, rows * top, most, skew, True), load_shares(number_of, rows * top, most, skew, False)
    places = jnp.arange(number_of)

    def named(lengths, rotation):
        used = int((lengths > 0).sum())
        fixed = max(1, used // 4)
        moved = fixed + (places - fixed + rotation * (used - fixed)) % max(1, number_of - fixed)
        return jnp.zeros((number_of,), jnp.int32).at[sequence[jnp.where(places < fixed, places, moved)]].set(jnp.asarray(lengths, jnp.int32))

    lengths = jnp.where(number % 4 == 0, named(packed, number // 4), named(ordinary, number - number // 4 - 1))
    mixed = jax.random.permutation(jax.random.fold_in(own, 3), number_of)
    source_of, sink = mixed[0:number_of // 2 * 2:2], mixed[1:number_of // 2 * 2:2]
    slack = jnp.minimum(lengths[source_of] - 1, most - lengths[sink]) // 2
    slack = jnp.where((source_of == sequence[0]) | (sink == sequence[0]) | (lengths[sink] == 0), 0, jnp.maximum(slack, 0))
    moved = jax.random.randint(jax.random.fold_in(own, 4), (number_of // 2,), 0, 1 << 20) % (slack + 1)
    lengths = lengths.at[source_of].add(-moved).at[sink].add(moved)
    items = jnp.searchsorted(jnp.cumsum(lengths), jnp.arange(rows * top), side="right").astype(jnp.int32)
    table = items.reshape(top, rows).T
    table = table[jax.random.permutation(jax.random.fold_in(own, 1), rows)]
    rotation = jax.random.randint(jax.random.fold_in(own, 2), (rows, 1), 0, top)
    return jnp.take_along_axis(table, (jnp.arange(top)[None, :] + rotation) % top, axis=1)


def load_shares(count, total, bound, skew, full):
    portions = [(1 << 20) // math.isqrt(standing ** skew) + 1 for standing in range(1, count + 1)]
    largest = bound if full else min(bound, max(-(-total // count), total * portions[0] // sum(portions)))
    least = 1 if total - largest >= count - 1 else 0
    given, spare = [largest] + [least] * (count - 1), total - largest - least * (count - 1)
    while spare > 0:
        movable = [i for i in range(1, count) if given[i] < largest] or [i for i in range(1, count) if given[i] < bound]
        mass, budget = sum([portions[i] for i in movable]), spare
        for i in movable:
            more = min(bound - given[i], max(1, budget * portions[i] // mass), spare)
            given[i] = given[i] + more
            spare = spare - more
    return np.array(given)


def scatter_about(key, shape, deviation, bound, split=(), kind=jnp.bfloat16):
    array = deviation * jax.random.normal(key, shape, jnp.float32)
    if split:
        array = array * levels(key, shape, split, -0.22, 0.18)
    return jnp.clip(array, -bound, bound).astype(kind)


def setup_inputs(seed: int = 0) -> dict:
    seeds = jax.random.split(jax.random.key(seed), 10)
    hidden = scatter_about(seeds[0], (ROWS, D), 1.0, 6.0, ((0, 32),))
    parents = place_ends(jax.random.randint(seeds[1], (ROWS,), 0, MICRO), jax.random.fold_in(seeds[1], 1), 0, MICRO - 1).astype(jnp.int32)
    routes_keys = jax.random.split(jax.random.fold_in(seeds[2], 1), ROWS // ROWS_DEV)
    routes_turns = jax.random.permutation(jax.random.fold_in(seeds[2], 3), ROWS // ROWS_DEV)
    routes = jax.vmap(lambda own, number: shared_out(jax.random.fold_in(seeds[2], 2), own, number, ROWS_DEV, EXPERTS, TOP, CAP, 1))(routes_keys, routes_turns).reshape((ROWS, TOP))
    gates = jnp.clip(0.05 + 0.95 * jax.random.uniform(seeds[3], (ROWS, TOP), jnp.float32) ** levels(seeds[3], (ROWS, TOP), ((0, 32),), -0.2, 0.2), 0.05, 1.0)
    counts = draw_counts(jax.random.fold_in(seeds[9], 71), 0)
    norm_gain = jnp.clip(1.0 + 0.18 * jax.random.normal(seeds[5], (D,), jnp.float32), 0.1, 1.9)
    w_gate = scatter_about(seeds[6], (EXPERTS, D, FFW), D ** -0.5, 0.09375, ((0, 32),))
    w_up = scatter_about(seeds[7], (EXPERTS, D, FFW), D ** -0.5, 0.09375, ((0, 32),))
    w_down = scatter_about(seeds[8], (EXPERTS, FFW, D), FFW ** -0.5, 0.21875, ((0, 32),))
    return {"hidden": hidden, "parents": parents, "routes": routes, "gates": gates, "counts": counts, "norm_gain": norm_gain, "w_gate": w_gate, "w_up": w_up, "w_down": w_down}


def reference(hidden, parents, routes, gates, counts, norm_gain, w_gate, w_up, w_down):
    micro = ROWS_DEV * N_EXP
    total_rows = hidden.shape[0]
    order = jnp.arange(total_rows, dtype=jnp.int32)
    source_row = (order // micro * micro + parents).astype(jnp.int32)
    picked = jnp.take(hidden, source_row, axis=0).astype(jnp.float32)
    scale = lax.rsqrt(lax.optimization_barrier(jnp.mean(picked * picked, axis=1, keepdims=True)) + 1e-06)
    normed = (picked * scale * norm_gain).astype(jnp.bfloat16)
    live = order % ROWS_DEV < jnp.take(counts, order // ROWS_DEV)
    weights = gates / lax.optimization_barrier(jnp.sum(gates, axis=1, keepdims=True)) * live[:, None].astype(gates.dtype)
    flat = routes.reshape(-1)
    slots = BLOCKS * CAP
    live_slot = jnp.repeat(live, TOP)
    onehot = ((flat[:, None] == jnp.arange(EXPERTS, dtype=jnp.int32)[None, :]) & live_slot[:, None]).astype(jnp.int32)
    before = jnp.cumsum(onehot, axis=0) - onehot
    rank = lax.optimization_barrier(jnp.sum(before * onehot, axis=1)).astype(jnp.int32)
    position = jnp.where(live_slot, flat * slots + rank, EXPERTS * slots).astype(jnp.int32)
    sentinel = total_rows * TOP
    table = jnp.full((EXPERTS * slots,), sentinel, jnp.int32)
    table = table.at[position].set(jnp.arange(sentinel, dtype=jnp.int32), mode='drop').reshape(EXPERTS, slots)
    flat_weights = weights.reshape(-1)

    def one_expert(accum, item):
        entry, gate_part, up_part, down_part = item
        valid = entry < sentinel
        safe = jnp.minimum(entry, sentinel - 1).astype(jnp.int32)
        rows_in = jnp.take(normed, safe // TOP, axis=0).astype(jnp.float32)
        gate_val = jnp.dot(rows_in, gate_part.astype(jnp.float32), precision=lax.Precision.HIGHEST)
        up_val = jnp.dot(rows_in, up_part.astype(jnp.float32), precision=lax.Precision.HIGHEST)
        act = (jax.nn.silu(gate_val) * up_val).astype(jnp.bfloat16)
        result = jnp.dot(act.astype(jnp.float32), down_part.astype(jnp.float32), precision=lax.Precision.HIGHEST).astype(jnp.bfloat16)
        share = jnp.where(valid, jnp.take(flat_weights, safe), jnp.zeros((), flat_weights.dtype))
        accum = accum.at[safe // TOP].add(share[:, None] * result.astype(jnp.float32))
        return (accum, None)
    mixed, _ = lax.scan(one_expert, jnp.zeros((total_rows, D), jnp.float32), (table, w_gate, w_up, w_down))
    return mixed.astype(jnp.bfloat16)
```

```python
import jax
import jax.numpy as jnp
from jax import lax
from jax.sharding import PartitionSpec as P

IN_CHUNKS = 4
OUT_CHUNKS = 4


def dot(a, b):
    return jnp.dot(a, b, preferred_element_type=jnp.float32)


def exchange(blocks, n_rep, back):
    moved = [blocks[0]]
    for step in range(1, n_rep):
        shift = n_rep - step if back else step
        pairs = [(i, (i + shift) % n_rep) for i in range(n_rep)]
        moved.append(lax.ppermute(blocks[step], "rep", pairs))
    return moved


def shards(hidden, parents, routes, gates, counts, norm_gain, w_gate, w_up, w_down):
    rows, width = hidden.shape
    top = routes.shape[1]
    n_rep = lax.axis_size("rep")
    n_exp = lax.axis_size("exp")
    cap = (rows * top // (n_rep * n_exp) + 2) * n_exp
    group = rows * n_exp
    my_rep = lax.axis_index("rep")
    my_exp = lax.axis_index("exp")
    bf16 = jnp.bfloat16

    live = jnp.arange(rows, dtype=jnp.int32) < counts[0]
    weights = gates / jnp.sum(gates, axis=1, keepdims=True) * live[:, None].astype(jnp.float32)
    named = jnp.where(live[:, None], routes, -1)
    facts = jnp.concatenate(
        [named.astype(jnp.float32), parents[:, None].astype(jnp.float32), weights], axis=1
    )
    facts = lax.all_gather(facts, "exp", axis=0, tiled=True)

    value = hidden.astype(jnp.float32)
    scale = lax.rsqrt(jnp.mean(value * value, axis=1, keepdims=True) + 1e-06)
    normed = (value * scale * norm_gain).astype(bf16)

    named = facts[:, :top].astype(jnp.int32)
    parent = facts[:, top].astype(jnp.int32)
    weights = facts[:, top + 1 :]
    expert = (my_rep + jnp.arange(n_rep, dtype=jnp.int32)) % n_rep * n_exp + my_exp
    hit = named[:, :, None] == expert[None, None, :]
    match = jnp.any(hit, axis=1)
    share = jnp.sum(jnp.where(hit, weights[:, :, None], 0.0), axis=1)
    earlier = (
        jnp.arange(group, dtype=jnp.int32)[:, None] > jnp.arange(group, dtype=jnp.int32)[None, :]
    )
    rank = dot(earlier.astype(bf16), match.astype(bf16)).astype(jnp.int32)
    rank = jnp.where(match, rank, -1)
    slot = jnp.arange(cap, dtype=jnp.int32)
    taken = rank.T[:, None, :] == slot[None, :, None]
    of_parent = (parent[:, None] == jnp.arange(group, dtype=jnp.int32)[None, :]).astype(bf16)
    select = dot(taken.reshape(n_rep * cap, group).astype(bf16), of_parent).astype(bf16)
    mix = jnp.where(rank[:, :, None] == slot[None, None, :], share[:, :, None], 0.0)
    mix = mix.reshape(group, n_rep * cap)
    mix_high = mix.astype(bf16)
    mix_low = (mix - mix_high.astype(jnp.float32)).astype(bf16)

    step = width // IN_CHUNKS
    gate_val = 0.0
    up_val = 0.0
    for part in range(IN_CHUNKS):
        cols = slice(part * step, (part + 1) * step)
        held = lax.all_gather(normed[:, cols], "exp", axis=0, tiled=True)
        blocks = [
            dot(select[s * cap : (s + 1) * cap], held).astype(bf16) for s in range(n_rep)
        ]
        arrived = jnp.concatenate(exchange(blocks, n_rep, False), axis=0)
        gate_val = gate_val + dot(arrived, w_gate[0, cols])
        up_val = up_val + dot(arrived, w_up[0, cols])
    act = (jax.nn.silu(gate_val) * up_val).astype(bf16)

    step = width // OUT_CHUNKS
    mixed = []
    for part in range(OUT_CHUNKS):
        cols = slice(part * step, (part + 1) * step)
        result = dot(act, w_down[0, :, cols]).astype(bf16)
        blocks = [result[s * cap : (s + 1) * cap] for s in range(n_rep)]
        returned = jnp.concatenate(exchange(blocks, n_rep, True), axis=0)
        partial = (dot(mix_high, returned) + dot(mix_low, returned)).astype(bf16)
        mixed.append(lax.psum_scatter(partial, "exp", scatter_dimension=0, tiled=True))
    return jnp.concatenate(mixed, axis=1)


def solution(mesh):
    placed = (
        P(("rep", "exp"), None),
        P(("rep", "exp")),
        P(("rep", "exp"), None),
        P(("rep", "exp"), None),
        P(("rep", "exp")),
        P(),
        P(("rep", "exp"), None, None),
        P(("rep", "exp"), None, None),
        P(("rep", "exp"), None, None),
    )
    return jax.shard_map(
        shards, mesh=mesh, in_specs=placed, out_specs=P(("rep", "exp"), None), check_vma=False
    )
```

```python
import functools

import jax
import jax.numpy as jnp
from jax import lax
from jax.experimental import pallas as pl
from jax.experimental.pallas import tpu as pltpu
from jax.sharding import PartitionSpec as P

IN_CHUNKS = 2
OUT_CHUNKS = 2
FACTS = 24
WEIGHT_ROW = 8
PARENT_ROW = 16
FITS_ROW = 17
BF16 = jnp.bfloat16


def dot(a, b):
    return jnp.dot(a, b, preferred_element_type=jnp.float32)


def dot_nt(a, b):
    return lax.dot_general(a, b, (((1,), (1,)), ((), ())), preferred_element_type=jnp.float32)


def dot_tn(a, b):
    return lax.dot_general(a, b, (((0,), (0,)), ((), ())), preferred_element_type=jnp.float32)


def round_up(value, unit):
    return -(-value // unit) * unit


def ring(value, axis, size, shift):
    if shift % size == 0:
        return value
    return lax.ppermute(value, axis, [(i, (i + shift) % size) for i in range(size)])


def flip(value, size, mask):
    if mask == 0:
        return value
    return lax.ppermute(value, "rep", [(i, i ^ mask) for i in range(size)])


def flat_iota(shape, dim):
    return lax.broadcasted_iota(jnp.int32, shape, dim)


def ones_where(condition):
    return jnp.where(condition, 1.0, 0.0).astype(BF16)


def any_hit(hits):
    return jnp.max(jnp.where(hits, 1.0, 0.0), axis=0, keepdims=True)


def parent_table(parent, group):
    return ones_where(flat_iota((group, group), 0) == parent.astype(jnp.int32))


def before_table(group, block):
    a = flat_iota((group, group), 0)
    b = flat_iota((group, group), 1)
    if block == group:
        return ones_where(a < b)
    low = b - lax.rem(b, block)
    return ones_where((a < b) & (a >= low))


def code_of(used, before):
    rank = dot(used.astype(BF16), before)
    return jnp.where(used > 0.5, rank + 1.0, 0.0)


def one_row(table, row):
    chosen = flat_iota(table.shape, 0) == row
    return jnp.sum(jnp.where(chosen, table, 0.0), axis=0, keepdims=True)


def slots_of(code, slots):
    return ones_where(flat_iota((slots, code.shape[1]), 0) + 1 == code.astype(jnp.int32))


def group_plan(sizes, place, facts, marked, pack, unpack, select, expand):
    n_rep, n_exp, rows, cap, cap_back, cap_z, cap_z_back = sizes
    group = rows * n_exp
    n_pair = n_rep // 2
    my_rep = place[0]
    my_exp = place[1]
    named = facts[0:8, :]
    parents = parent_table(facts[PARENT_ROW : PARENT_ROW + 1, :], group)
    in_block = before_table(group, rows)
    in_group = before_table(group, group)

    lane = named - jnp.floor((named + 0.5) / n_exp) * n_exp
    planes = [any_hit((lane == float(z)) & (named >= 0.0)) for z in range(n_exp)]
    planes = jnp.concatenate(planes + [jnp.zeros_like(planes[0])] * (-n_exp % 8), axis=0)
    wanted = jnp.where(dot_nt(planes.astype(BF16), parents) > 0.5, 1.0, 0.0)
    code_z = code_of(wanted, in_block)
    code_z_back = code_of(planes, in_block)

    column = flat_iota((1, group), 1)
    block_of = lax.div(column, rows)
    turn = lax.rem(my_exp - block_of + n_exp, n_exp)

    def own_block(table):
        total = jnp.zeros((table.shape[0], rows), jnp.float32)
        for b in range(n_exp):
            part = table[:, b * rows : (b + 1) * rows]
            total = total + jnp.where(my_exp == b, part, 0.0)
        return total

    mine = own_block(code_z)
    mine_back = own_block(code_z_back)
    for s in range(n_exp):
        plane = lax.rem(my_exp + s, n_exp)
        pack[s * cap_z : (s + 1) * cap_z, :] = slots_of(one_row(mine, plane), cap_z)
        unpack[s * cap_z_back : (s + 1) * cap_z_back, :] = slots_of(
            one_row(mine_back, plane), cap_z_back
        )

    def packed(code, slots):
        code = one_row(code, my_exp)
        held = (code > 0.5) & (code < slots + 0.5)
        where = jnp.where(held, turn.astype(jnp.float32) * slots + code, 0.0)
        return slots_of(where, n_exp * slots)

    held = packed(code_z, cap_z)
    held_back = packed(code_z_back, cap_z_back)

    visits = []
    for pair in range(n_pair):
        for z in range(n_exp):
            first = float(2 * pair * n_exp + z)
            visits.append(any_hit((named == first) | (named == first + n_exp)))
    visits = jnp.concatenate(visits + [jnp.zeros_like(visits[0])] * (-len(visits) % 8), axis=0)
    needs = jnp.where(dot_nt(visits.astype(BF16), parents) > 0.5, 1.0, 0.0)
    code = code_of(needs, in_group)
    code_back = code_of(visits, in_group)
    for k in range(n_pair):
        pair = lax.div(lax.bitwise_xor(my_rep, 2 * k), 2)
        row = pair * n_exp + my_exp
        chosen = slots_of(one_row(code, row), cap)
        select[k * cap : (k + 1) * cap, :] = dot_nt(chosen, held).astype(BF16)
        chosen = slots_of(one_row(code_back, row), cap_back)
        expand[:, k * cap_back : (k + 1) * cap_back] = dot_nt(held_back, chosen).astype(BF16)

    over = jnp.maximum(jnp.max(code_z) - cap_z, jnp.max(code_z_back) - cap_z_back)
    over = jnp.maximum(over, jnp.max(code) - cap)
    over = jnp.maximum(over, jnp.max(code_back) - cap_back)
    marked[...] = facts[...]
    marked[FITS_ROW : FITS_ROW + 1, :] = jnp.where(over > 0.5, 0.0, 1.0) * jnp.ones((1, group))


def pair_plan(sizes, place, facts, high, low):
    n_rep, n_exp, rows, cap, cap_back, cap_z, cap_z_back = sizes
    group = rows * n_exp
    n_pair = n_rep // 2
    my_rep = place[0]
    my_exp = place[1]
    in_group = before_table(group, group)
    own = my_rep * n_exp + my_exp
    other = lax.bitwise_xor(my_rep, 1) * n_exp + my_exp
    for k in range(n_pair):
        named = facts[k * FACTS : k * FACTS + 8, :].astype(jnp.int32)
        weights = facts[k * FACTS + WEIGHT_ROW : k * FACTS + WEIGHT_ROW + 8, :]
        parents = parent_table(facts[k * FACTS + PARENT_ROW : k * FACTS + PARENT_ROW + 1, :], group)
        visit = any_hit((named == own) | (named == other)) * jnp.ones((8, 1), jnp.float32)
        needs = jnp.where(dot_nt(visit.astype(BF16), parents) > 0.5, 1.0, 0.0)
        code = code_of(needs, in_group)[0:1, :]
        code_back = code_of(visit, in_group)[0:1, :]
        source = dot(slots_of(code, cap), parents).astype(BF16)
        target = slots_of(code_back, cap_back).astype(jnp.float32)
        for at, expert in enumerate((own, other)):
            weight = jnp.sum(jnp.where(named == expert, weights, 0.0), axis=0, keepdims=True)
            weight_high = weight.astype(BF16).astype(jnp.float32)
            for out, value in ((high, weight_high), (low, weight - weight_high)):
                table = dot_nt((target * value).astype(BF16), source).astype(BF16)
                out[k * cap_back : (k + 1) * cap_back, at * cap : (at + 1) * cap] = table


def plan_call(body, sizes, shapes, place, facts):
    whole = pl.BlockSpec(memory_space=pltpu.VMEM)
    return pl.pallas_call(
        functools.partial(body, sizes),
        out_shape=[jax.ShapeDtypeStruct(shape, kind) for shape, kind in shapes],
        in_specs=[pl.BlockSpec(memory_space=pltpu.SMEM), whole],
        out_specs=[whole] * len(shapes),
        compiler_params=pltpu.CompilerParams(vmem_limit_bytes=48 * 1024 * 1024),
    )(place, facts)


def shards(hidden, parents, routes, gates, counts, norm_gain, w_gate, w_up, w_down):
    rows, width = hidden.shape
    top = routes.shape[1]
    n_rep = lax.axis_size("rep")
    n_exp = lax.axis_size("exp")
    n_pair = n_rep // 2
    group = rows * n_exp
    my_rep = lax.axis_index("rep")
    my_exp = lax.axis_index("exp")
    most = (rows * top // (n_rep * n_exp) + 2) * n_exp
    cap = round_up(most + most // 8, 16)
    cap_back = round_up(most + most // 4, 16)
    cap_z = rows // 2
    cap_z_back = rows // 2
    sizes = (n_rep, n_exp, rows, cap, cap_back, cap_z, cap_z_back)
    place = jnp.stack([my_rep, my_exp]).astype(jnp.int32)

    live = (jnp.arange(rows, dtype=jnp.int32) < counts[0])[None, :]
    scores = gates.T
    weights = scores / jnp.sum(scores, axis=0, keepdims=True) * live.astype(jnp.float32)
    named = jnp.where(live, routes.T, -1).astype(jnp.float32)
    parent = parents[None, :].astype(jnp.float32)
    filler = jnp.zeros((FACTS - PARENT_ROW - 1, rows), jnp.float32)
    own_facts = jnp.concatenate([named, weights, parent, filler], axis=0)
    gathered = [own_facts] + [ring(own_facts, "exp", n_exp, s) for s in range(1, n_exp)]
    order = lax.rem(my_exp - jnp.arange(n_exp, dtype=jnp.int32) + n_exp, n_exp)
    arranged = [
        sum(jnp.where(order[b] == s, gathered[s], 0.0) for s in range(n_exp)) for b in range(n_exp)
    ]
    facts = jnp.concatenate(arranged, axis=1)

    value = hidden.astype(jnp.float32)
    scale = lax.rsqrt(jnp.mean(value * value, axis=1, keepdims=True) + 1e-06)
    normed = (value * scale * norm_gain).astype(BF16)

    marked, pack, unpack, select, expand = plan_call(
        group_plan,
        sizes,
        [
            ((FACTS, group), jnp.float32),
            ((n_exp * cap_z, rows), BF16),
            ((n_exp * cap_z_back, rows), BF16),
            ((n_pair * cap, n_exp * cap_z), BF16),
            ((n_exp * cap_z_back, n_pair * cap_back), BF16),
        ],
        place,
        facts,
    )

    in_step = width // IN_CHUNKS
    out_step = width // OUT_CHUNKS

    def along_exp(part):
        cols = slice(part * in_step, (part + 1) * in_step)
        sent = [
            dot(pack[s * cap_z : (s + 1) * cap_z], normed[:, cols]).astype(BF16)
            for s in range(n_exp)
        ]
        return [ring(sent[s], "exp", n_exp, s) for s in range(n_exp)]

    first = along_exp(0)
    others = [flip(marked, n_rep, mask) for mask in range(n_rep)]
    fits = functools.reduce(jnp.minimum, [other[FITS_ROW, 0] for other in others])
    served = jnp.concatenate([others[2 * k] for k in range(n_pair)], axis=0)

    def compact(first, normed, served, facts):
        high, low = plan_call(
            pair_plan, sizes, [((n_pair * cap_back, 2 * cap), BF16)] * 2, place, served
        )
        sums = [0.0] * 4
        for part in range(IN_CHUNKS):
            cols = slice(part * in_step, (part + 1) * in_step)
            held = jnp.concatenate(first if part == 0 else along_exp(part), axis=0)
            sent = [
                dot(select[k * cap : (k + 1) * cap], held).astype(BF16) for k in range(n_pair)
            ]
            arrived = jnp.concatenate([flip(sent[k], n_rep, 2 * k) for k in range(n_pair)], axis=0)
            swapped = flip(arrived, n_rep, 1)
            sums[0] = sums[0] + dot(arrived, w_gate[0, cols])
            sums[1] = sums[1] + dot(arrived, w_up[0, cols])
            sums[2] = sums[2] + dot(swapped, w_gate[0, cols])
            sums[3] = sums[3] + dot(swapped, w_up[0, cols])
        act_own = (jax.nn.silu(sums[0]) * sums[1]).astype(BF16)
        act_other = (jax.nn.silu(sums[2]) * sums[3]).astype(BF16)
        mixed = []
        for part in range(OUT_CHUNKS):
            cols = slice(part * out_step, (part + 1) * out_step)
            given = flip(dot(act_other, w_down[0, :, cols]).astype(BF16), n_rep, 1)
            own = dot(act_own, w_down[0, :, cols]).astype(BF16)
            returned = []
            for k in range(n_pair):
                at = slice(k * cap, (k + 1) * cap)
                both = jnp.concatenate([own[at], given[at]], axis=0)
                to = slice(k * cap_back, (k + 1) * cap_back)
                total = (dot(high[to], both) + dot(low[to], both)).astype(BF16)
                returned.append(flip(total, n_rep, 2 * k))
            partial = dot(expand, jnp.concatenate(returned, axis=0)).astype(BF16)
            blocks = [
                ring(partial[s * cap_z_back : (s + 1) * cap_z_back], "exp", n_exp, -s)
                for s in range(n_exp)
            ]
            mixed.append(dot_tn(unpack, jnp.concatenate(blocks, axis=0)).astype(BF16))
        return jnp.concatenate(mixed, axis=1)

    def full(first, normed, served, facts):
        return full_capacity(normed, facts, most, w_gate, w_up, w_down)

    return lax.cond(fits > 0.5, compact, full, first, normed, served, facts)


def full_capacity(normed, facts, cap, w_gate, w_up, w_down):
    rows, width = normed.shape
    n_rep = lax.axis_size("rep")
    n_exp = lax.axis_size("exp")
    group = rows * n_exp
    my_rep = lax.axis_index("rep")
    my_exp = lax.axis_index("exp")
    named = facts[:8].T.astype(jnp.int32)
    weights = facts[WEIGHT_ROW : WEIGHT_ROW + 8].T
    parent = facts[PARENT_ROW].astype(jnp.int32)
    expert = (my_rep + jnp.arange(n_rep, dtype=jnp.int32)) % n_rep * n_exp + my_exp
    hit = named[:, :, None] == expert[None, None, :]
    match = jnp.any(hit, axis=1)
    share = jnp.sum(jnp.where(hit, weights[:, :, None], 0.0), axis=1)
    item = jnp.arange(group, dtype=jnp.int32)
    rank = dot((item[:, None] > item[None, :]).astype(BF16), match.astype(BF16)).astype(jnp.int32)
    rank = jnp.where(match, rank, -1)
    slot = jnp.arange(cap, dtype=jnp.int32)
    taken = rank.T[:, None, :] == slot[None, :, None]
    of_parent = (parent[:, None] == item[None, :]).astype(BF16)
    select = dot(taken.reshape(n_rep * cap, group).astype(BF16), of_parent).astype(BF16)
    mix = jnp.where(rank[:, :, None] == slot[None, None, :], share[:, :, None], 0.0)
    mix = mix.reshape(group, n_rep * cap)
    mix_high = mix.astype(BF16)
    mix_low = (mix - mix_high.astype(jnp.float32)).astype(BF16)

    step = width // 4
    gate_val = 0.0
    up_val = 0.0
    for part in range(4):
        cols = slice(part * step, (part + 1) * step)
        held = lax.all_gather(normed[:, cols], "exp", axis=0, tiled=True)
        moved = [
            ring(dot(select[s * cap : (s + 1) * cap], held).astype(BF16), "rep", n_rep, s)
            for s in range(n_rep)
        ]
        arrived = jnp.concatenate(moved, axis=0)
        gate_val = gate_val + dot(arrived, w_gate[0, cols])
        up_val = up_val + dot(arrived, w_up[0, cols])
    act = (jax.nn.silu(gate_val) * up_val).astype(BF16)
    mixed = []
    for part in range(4):
        cols = slice(part * step, (part + 1) * step)
        result = dot(act, w_down[0, :, cols]).astype(BF16)
        moved = [ring(result[s * cap : (s + 1) * cap], "rep", n_rep, -s) for s in range(n_rep)]
        returned = jnp.concatenate(moved, axis=0)
        partial = (dot(mix_high, returned) + dot(mix_low, returned)).astype(BF16)
        mixed.append(lax.psum_scatter(partial, "exp", scatter_dimension=0, tiled=True))
    return jnp.concatenate(mixed, axis=1)


def solution(mesh):
    placed = (
        P(("rep", "exp"), None),
        P(("rep", "exp")),
        P(("rep", "exp"), None),
        P(("rep", "exp"), None),
        P(("rep", "exp")),
        P(),
        P(("rep", "exp"), None, None),
        P(("rep", "exp"), None, None),
        P(("rep", "exp"), None, None),
    )
    return jax.shard_map(
        shards, mesh=mesh, in_specs=placed, out_specs=P(("rep", "exp"), None), check_vma=False
    )
```

```python
import functools

import jax
import jax.numpy as jnp
from jax import lax
from jax.experimental import pallas as pl
from jax.experimental.pallas import tpu as pltpu
from jax.sharding import PartitionSpec as P

IN_PARTS = (2, 3, 3)
OUT_PARTS = (3, 3, 2)
FACTS = 24
WEIGHT_ROW = 8
PARENT_ROW = 16
FITS_ROW = 17
BF16 = jnp.bfloat16


def dot(a, b):
    return jnp.dot(a, b, preferred_element_type=jnp.float32)


def dot_nt(a, b):
    return lax.dot_general(a, b, (((1,), (1,)), ((), ())), preferred_element_type=jnp.float32)


def dot_tn(a, b):
    return lax.dot_general(a, b, (((0,), (0,)), ((), ())), preferred_element_type=jnp.float32)


def round_up(value, unit):
    return -(-value // unit) * unit


def ring(value, axis, size, shift):
    if shift % size == 0:
        return value
    return lax.ppermute(value, axis, [(i, (i + shift) % size) for i in range(size)])


def flip(value, size, mask):
    if mask == 0:
        return value
    return lax.ppermute(value, "rep", [(i, i ^ mask) for i in range(size)])


def flat_iota(shape, dim):
    return lax.broadcasted_iota(jnp.int32, shape, dim)


def ones_where(condition):
    return jnp.where(condition, 1.0, 0.0).astype(BF16)


def any_hit(hits):
    return jnp.max(jnp.where(hits, 1.0, 0.0), axis=0, keepdims=True)


def parent_table(parent, group):
    return ones_where(flat_iota((group, group), 0) == parent.astype(jnp.int32))


def before_table(group, block):
    a = flat_iota((group, group), 0)
    b = flat_iota((group, group), 1)
    if block == group:
        return ones_where(a < b)
    low = b - lax.rem(b, block)
    return ones_where((a < b) & (a >= low))


def code_of(used, before):
    rank = dot(used.astype(BF16), before)
    return jnp.where(used > 0.5, rank + 1.0, 0.0)


def one_row(table, row):
    chosen = flat_iota(table.shape, 0) == row
    return jnp.sum(jnp.where(chosen, table, 0.0), axis=0, keepdims=True)


def slots_of(code, slots):
    return ones_where(flat_iota((slots, code.shape[1]), 0) + 1 == code.astype(jnp.int32))


def own_facts(counts, routes, gates, parents, facts):
    column = flat_iota((1, routes.shape[1]), 1)
    live = column < counts[0]
    scores = gates[...]
    weights = scores / jnp.sum(scores, axis=0, keepdims=True) * jnp.where(live, 1.0, 0.0)
    facts[...] = jnp.zeros_like(facts)
    facts[0:8, :] = jnp.where(live, routes[...], -1).astype(jnp.float32)
    facts[WEIGHT_ROW : WEIGHT_ROW + 8, :] = weights
    facts[PARENT_ROW : PARENT_ROW + 1, :] = parents[...].astype(jnp.float32)


def group_plan(sizes, place, *refs):
    n_rep, n_exp, rows, cap, cap_back, cap_z, cap_z_back = sizes
    blocks = refs[:n_exp]
    facts, pack, unpack, select, expand = refs[n_exp:]
    group = rows * n_exp
    n_pair = n_rep // 2
    my_rep = place[0]
    my_exp = place[1]
    for s in range(n_exp):
        facts[:, s * rows : (s + 1) * rows] = blocks[s][...]
    named = facts[0:8, :]
    parent = facts[PARENT_ROW : PARENT_ROW + 1, :].astype(jnp.int32)
    block = lax.div(parent, rows)
    parent = parent + (lax.rem(my_exp - block + n_exp, n_exp) - block) * rows
    facts[PARENT_ROW : PARENT_ROW + 1, :] = parent.astype(jnp.float32)
    parents = parent_table(parent, group)
    in_block = before_table(group, rows)
    in_group = before_table(group, group)

    lane = named - jnp.floor((named + 0.5) / n_exp) * n_exp
    planes = [any_hit((lane == float(z)) & (named >= 0.0)) for z in range(n_exp)]
    planes = jnp.concatenate(planes + [jnp.zeros_like(planes[0])] * (-n_exp % 8), axis=0)
    wanted = jnp.where(dot_nt(planes.astype(BF16), parents) > 0.5, 1.0, 0.0)
    code_z = code_of(wanted, in_block)
    code_z_back = code_of(planes, in_block)
    for s in range(n_exp):
        plane = lax.rem(my_exp + s, n_exp)
        pack[s * cap_z : (s + 1) * cap_z, :] = slots_of(one_row(code_z[:, :rows], plane), cap_z)
        unpack[s * cap_z_back : (s + 1) * cap_z_back, :] = slots_of(
            one_row(code_z_back[:, :rows], plane), cap_z_back
        )

    turn = lax.div(flat_iota((1, group), 1), rows).astype(jnp.float32)

    def packed(code, slots):
        code = one_row(code, my_exp)
        held = (code > 0.5) & (code < slots + 0.5)
        return slots_of(jnp.where(held, turn * slots + code, 0.0), n_exp * slots)

    held = packed(code_z, cap_z)
    held_back = packed(code_z_back, cap_z_back)

    visits = []
    for pair in range(n_pair):
        for z in range(n_exp):
            first = float(2 * pair * n_exp + z)
            visits.append(any_hit((named == first) | (named == first + n_exp)))
    visits = jnp.concatenate(visits + [jnp.zeros_like(visits[0])] * (-len(visits) % 8), axis=0)
    needs = jnp.where(dot_nt(visits.astype(BF16), parents) > 0.5, 1.0, 0.0)
    code = code_of(needs, in_group)
    code_back = code_of(visits, in_group)
    for k in range(n_pair):
        pair = lax.div(lax.bitwise_xor(my_rep, 2 * k), 2)
        row = pair * n_exp + my_exp
        chosen = slots_of(one_row(code, row), cap)
        select[k * cap : (k + 1) * cap, :] = dot_nt(chosen, held).astype(BF16)
        chosen = slots_of(one_row(code_back, row), cap_back)
        expand[:, k * cap_back : (k + 1) * cap_back] = dot_nt(held_back, chosen).astype(BF16)

    over = jnp.maximum(jnp.max(code_z) - cap_z, jnp.max(code_z_back) - cap_z_back)
    over = jnp.maximum(over, jnp.max(code) - cap)
    over = jnp.maximum(over, jnp.max(code_back) - cap_back)
    facts[FITS_ROW : FITS_ROW + 1, :] = jnp.where(over > 0.5, 0.0, 1.0) * jnp.ones((1, group))


def pair_plan(sizes, place, *refs):
    n_rep, n_exp, rows, cap, cap_back, cap_z, cap_z_back = sizes
    group = rows * n_exp
    n_pair = n_rep // 2
    high, low = refs[n_pair:]
    my_rep = place[0]
    my_exp = place[1]
    in_group = before_table(group, group)
    own = my_rep * n_exp + my_exp
    other = lax.bitwise_xor(my_rep, 1) * n_exp + my_exp
    for k in range(n_pair):
        named = refs[k][0:8, :].astype(jnp.int32)
        weights = refs[k][WEIGHT_ROW : WEIGHT_ROW + 8, :]
        parents = parent_table(refs[k][PARENT_ROW : PARENT_ROW + 1, :], group)
        visit = any_hit((named == own) | (named == other)) * jnp.ones((8, 1), jnp.float32)
        needs = jnp.where(dot_nt(visit.astype(BF16), parents) > 0.5, 1.0, 0.0)
        code = code_of(needs, in_group)[0:1, :]
        code_back = code_of(visit, in_group)[0:1, :]
        source = dot(slots_of(code, cap), parents).astype(BF16)
        target = slots_of(code_back, cap_back).astype(jnp.float32)
        for at, expert in enumerate((own, other)):
            weight = jnp.sum(jnp.where(named == expert, weights, 0.0), axis=0, keepdims=True)
            weight_high = weight.astype(BF16).astype(jnp.float32)
            for out, value in ((high, weight_high), (low, weight - weight_high)):
                table = dot_nt((target * value).astype(BF16), source).astype(BF16)
                out[k * cap_back : (k + 1) * cap_back, at * cap : (at + 1) * cap] = table


def plan_call(body, shapes, place, *tables):
    whole = pl.BlockSpec(memory_space=pltpu.VMEM)
    return pl.pallas_call(
        body,
        out_shape=[jax.ShapeDtypeStruct(shape, kind) for shape, kind in shapes],
        in_specs=[pl.BlockSpec(memory_space=pltpu.SMEM)] + [whole] * len(tables),
        out_specs=[whole] * len(shapes),
        compiler_params=pltpu.CompilerParams(vmem_limit_bytes=48 * 1024 * 1024),
    )(place, *tables)


def column_parts(width, parts):
    unit = width // sum(parts)
    ends = [unit * sum(parts[: i + 1]) for i in range(len(parts))]
    return [slice(end - unit * part, end) for part, end in zip(parts, ends)]


def shards(hidden, parents, routes, gates, counts, norm_gain, w_gate, w_up, w_down):
    rows, width = hidden.shape
    top = routes.shape[1]
    n_rep = lax.axis_size("rep")
    n_exp = lax.axis_size("exp")
    n_pair = n_rep // 2
    group = rows * n_exp
    my_rep = lax.axis_index("rep")
    my_exp = lax.axis_index("exp")
    most = (rows * top // (n_rep * n_exp) + 2) * n_exp
    cap = round_up(most + most // 8, 16)
    cap_back = round_up(most + most // 4, 16)
    cap_z = rows // 2
    cap_z_back = rows // 2
    sizes = (n_rep, n_exp, rows, cap, cap_back, cap_z, cap_z_back)
    place = jnp.stack([my_rep, my_exp]).astype(jnp.int32)

    (own,) = plan_call(
        own_facts,
        [((FACTS, rows), jnp.float32)],
        counts,
        routes.T,
        gates.T,
        parents[None, :],
    )
    blocks = [ring(own, "exp", n_exp, s) for s in range(n_exp)]

    value = hidden.astype(jnp.float32)
    scale = lax.rsqrt(jnp.mean(value * value, axis=1, keepdims=True) + 1e-06)
    normed = (value * scale * norm_gain).astype(BF16)

    facts, pack, unpack, select, expand = plan_call(
        functools.partial(group_plan, sizes),
        [
            ((FACTS, group), jnp.float32),
            ((n_exp * cap_z, rows), BF16),
            ((n_exp * cap_z_back, rows), BF16),
            ((n_pair * cap, n_exp * cap_z), BF16),
            ((n_exp * cap_z_back, n_pair * cap_back), BF16),
        ],
        place,
        *blocks,
    )
    served = [flip(facts, n_rep, 2 * k) for k in range(n_pair)]
    fits = functools.reduce(jnp.minimum, [other[PARENT_ROW:, : 128] for other in served])
    fits = jnp.minimum(fits, flip(fits, n_rep, 1))
    high, low = plan_call(
        functools.partial(pair_plan, sizes),
        [((n_pair * cap_back, 2 * cap), BF16)] * 2,
        place,
        *served,
    )

    def along_exp(cols):
        sent = [
            dot(pack[s * cap_z : (s + 1) * cap_z], normed[:, cols]).astype(BF16)
            for s in range(n_exp)
        ]
        return [ring(sent[s], "exp", n_exp, s) for s in range(n_exp)]

    in_cols = column_parts(width, IN_PARTS)
    sums = (0.0, 0.0, 0.0, 0.0)
    held = along_exp(in_cols[0])
    for part, cols in enumerate(in_cols):
        held = jnp.concatenate(held, axis=0)
        sent = [dot(select[k * cap : (k + 1) * cap], held).astype(BF16) for k in range(n_pair)]
        moved = [flip(sent[k], n_rep, 2 * k) for k in range(n_pair)]
        held = along_exp(in_cols[part + 1]) if part + 1 < len(in_cols) else None
        moved, held, sums, high, low, fits = lax.optimization_barrier(
            (moved, held, sums, high, low, fits)
        )
        arrived = jnp.concatenate(moved, axis=0)
        swapped = flip(arrived, n_rep, 1)
        sums = (
            sums[0] + dot(arrived, w_gate[0, cols]),
            sums[1] + dot(arrived, w_up[0, cols]),
            sums[2] + dot(swapped, w_gate[0, cols]),
            sums[3] + dot(swapped, w_up[0, cols]),
        )
    act_own = (jax.nn.silu(sums[0]) * sums[1]).astype(BF16)
    act_other = (jax.nn.silu(sums[2]) * sums[3]).astype(BF16)

    def weighted(cols, act_own, act_other):
        given = flip(dot(act_other, w_down[0, :, cols]).astype(BF16), n_rep, 1)
        own = dot(act_own, w_down[0, :, cols]).astype(BF16)
        totals = []
        for k in range(n_pair):
            at = slice(k * cap, (k + 1) * cap)
            both = jnp.concatenate([own[at], given[at]], axis=0)
            to = slice(k * cap_back, (k + 1) * cap_back)
            totals.append((dot(high[to], both) + dot(low[to], both)).astype(BF16))
        return totals

    out_cols = column_parts(width, OUT_PARTS)
    parts = []
    totals = weighted(out_cols[0], act_own, act_other)
    blocks = None
    for part, cols in enumerate(out_cols):
        totals, act_own, act_other = lax.optimization_barrier((totals, act_own, act_other))
        returned = [flip(totals[k], n_rep, 2 * k) for k in range(n_pair)]
        if part + 1 < len(out_cols):
            totals = weighted(out_cols[part + 1], act_own, act_other)
        returned, totals, blocks = lax.optimization_barrier((returned, totals, blocks))
        if part:
            parts.append(blocks)
        partial = dot(expand, jnp.concatenate(returned, axis=0)).astype(BF16)
        blocks = [
            ring(partial[s * cap_z_back : (s + 1) * cap_z_back], "exp", n_exp, -s)
            for s in range(n_exp)
        ]
    parts.append(blocks)

    def compact(parts, normed, facts, w_gate, w_up, w_down):
        mixed = [dot_tn(unpack, jnp.concatenate(part, axis=0)).astype(BF16) for part in parts]
        return jnp.concatenate(mixed, axis=1)

    def full(parts, normed, facts, w_gate, w_up, w_down):
        return full_capacity(normed, facts, most, w_gate, w_up, w_down)

    return lax.cond(
        fits[FITS_ROW - PARENT_ROW, 0] > 0.5,
        compact,
        full,
        parts,
        normed,
        facts,
        w_gate,
        w_up,
        w_down,
    )


def full_capacity(normed, facts, cap, w_gate, w_up, w_down):
    rows, width = normed.shape
    n_rep = lax.axis_size("rep")
    n_exp = lax.axis_size("exp")
    group = rows * n_exp
    my_rep = lax.axis_index("rep")
    my_exp = lax.axis_index("exp")
    named = facts[:8].T.astype(jnp.int32)
    weights = facts[WEIGHT_ROW : WEIGHT_ROW + 8].T
    parent = facts[PARENT_ROW].astype(jnp.int32)
    expert = (my_rep + jnp.arange(n_rep, dtype=jnp.int32)) % n_rep * n_exp + my_exp
    hit = named[:, :, None] == expert[None, None, :]
    match = jnp.any(hit, axis=1)
    share = jnp.sum(jnp.where(hit, weights[:, :, None], 0.0), axis=1)
    item = jnp.arange(group, dtype=jnp.int32)
    rank = dot((item[:, None] > item[None, :]).astype(BF16), match.astype(BF16)).astype(jnp.int32)
    rank = jnp.where(match, rank, -1)
    slot = jnp.arange(cap, dtype=jnp.int32)
    taken = rank.T[:, None, :] == slot[None, :, None]
    of_parent = (parent[:, None] == item[None, :]).astype(BF16)
    select = dot(taken.reshape(n_rep * cap, group).astype(BF16), of_parent).astype(BF16)
    mix = jnp.where(rank[:, :, None] == slot[None, None, :], share[:, :, None], 0.0)
    mix = mix.reshape(group, n_rep * cap)
    mix_high = mix.astype(BF16)
    mix_low = (mix - mix_high.astype(jnp.float32)).astype(BF16)

    held = jnp.concatenate([ring(normed, "exp", n_exp, s) for s in range(n_exp)], axis=0)
    moved = [
        ring(dot(select[s * cap : (s + 1) * cap], held).astype(BF16), "rep", n_rep, s)
        for s in range(n_rep)
    ]
    arrived = jnp.concatenate(moved, axis=0)
    act = (jax.nn.silu(dot(arrived, w_gate[0])) * dot(arrived, w_up[0])).astype(BF16)
    result = dot(act, w_down[0]).astype(BF16)
    moved = [ring(result[s * cap : (s + 1) * cap], "rep", n_rep, -s) for s in range(n_rep)]
    returned = jnp.concatenate(moved, axis=0)
    partial = (dot(mix_high, returned) + dot(mix_low, returned)).astype(BF16)
    mixed = jnp.zeros((rows, width), jnp.float32)
    for s in range(n_exp):
        mixed = mixed + ring(partial[s * rows : (s + 1) * rows], "exp", n_exp, -s)
    return mixed.astype(BF16)


def solution(mesh):
    placed = (
        P(("rep", "exp"), None),
        P(("rep", "exp")),
        P(("rep", "exp"), None),
        P(("rep", "exp"), None),
        P(("rep", "exp")),
        P(),
        P(("rep", "exp"), None, None),
        P(("rep", "exp"), None, None),
        P(("rep", "exp"), None, None),
    )
    return jax.shard_map(
        shards, mesh=mesh, in_specs=placed, out_specs=P(("rep", "exp"), None), check_vma=False
    )
```

```python
import functools

import jax
import jax.numpy as jnp
from jax import lax
from jax.experimental import pallas as pl
from jax.experimental.pallas import tpu as pltpu
from jax.sharding import PartitionSpec as P

IN_PARTS = (4, 7, 5)
OUT_PARTS = (4, 7, 5)
FACTS = 24
WEIGHT_ROW = 8
PARENT_ROW = 16
FITS_ROW = 17
BF16 = jnp.bfloat16


def dot(a, b):
    return jnp.dot(a, b, preferred_element_type=jnp.float32)


def dot_nt(a, b):
    return lax.dot_general(a, b, (((1,), (1,)), ((), ())), preferred_element_type=jnp.float32)


def dot_tn(a, b):
    return lax.dot_general(a, b, (((0,), (0,)), ((), ())), preferred_element_type=jnp.float32)


def round_up(value, unit):
    return -(-value // unit) * unit


def ring(value, axis, size, shift):
    if shift % size == 0:
        return value
    return lax.ppermute(value, axis, [(i, (i + shift) % size) for i in range(size)])


def flip(value, size, mask):
    if mask == 0:
        return value
    return lax.ppermute(value, "rep", [(i, i ^ mask) for i in range(size)])


def flat_iota(shape, dim):
    return lax.broadcasted_iota(jnp.int32, shape, dim)


def ones_where(condition):
    return jnp.where(condition, 1.0, 0.0).astype(BF16)


def any_hit(hits):
    return jnp.max(jnp.where(hits, 1.0, 0.0), axis=0, keepdims=True)


def parent_table(parent, group):
    return ones_where(flat_iota((group, group), 0) == parent.astype(jnp.int32))


def before_table(group, block):
    a = flat_iota((group, group), 0)
    b = flat_iota((group, group), 1)
    if block == group:
        return ones_where(a < b)
    low = b - lax.rem(b, block)
    return ones_where((a < b) & (a >= low))


def code_of(used, before):
    rank = dot(used.astype(BF16), before)
    return jnp.where(used > 0.5, rank + 1.0, 0.0)


def one_row(table, row):
    chosen = flat_iota(table.shape, 0) == row
    return jnp.sum(jnp.where(chosen, table, 0.0), axis=0, keepdims=True)


def slots_of(code, slots):
    return ones_where(flat_iota((slots, code.shape[1]), 0) + 1 == code.astype(jnp.int32))


def own_facts(given, routes, gates, parents, facts):
    column = flat_iota((1, routes.shape[1]), 1)
    live = (column < given[0]) & (lax.rem(column, given[1]) == given[2])
    scores = gates[...]
    weights = scores / jnp.sum(scores, axis=0, keepdims=True) * jnp.where(live, 1.0, 0.0)
    facts[...] = jnp.zeros_like(facts)
    facts[0:8, :] = jnp.where(live, routes[...], -1).astype(jnp.float32)
    facts[WEIGHT_ROW : WEIGHT_ROW + 8, :] = weights
    facts[PARENT_ROW : PARENT_ROW + 1, :] = parents[...].astype(jnp.float32)


def group_plan(sizes, place, *refs):
    n_rep, n_exp, rows, cap, cap_back, cap_z, cap_z_back = sizes
    blocks = refs[:n_exp]
    facts, pack, unpack, select, expand = refs[n_exp:]
    group = rows * n_exp
    n_pair = n_rep // 2
    my_rep = place[0]
    my_exp = place[1]
    for s in range(n_exp):
        facts[:, s * rows : (s + 1) * rows] = blocks[s][...]
    named = facts[0:8, :]
    parent = facts[PARENT_ROW : PARENT_ROW + 1, :].astype(jnp.int32)
    block = lax.div(parent, rows)
    parent = parent + (lax.rem(my_exp - block + n_exp, n_exp) - block) * rows
    facts[PARENT_ROW : PARENT_ROW + 1, :] = parent.astype(jnp.float32)
    parents = parent_table(parent, group)
    in_block = before_table(group, rows)
    in_group = before_table(group, group)

    lane = named - jnp.floor((named + 0.5) / n_exp) * n_exp
    planes = [any_hit((lane == float(z)) & (named >= 0.0)) for z in range(n_exp)]
    planes = jnp.concatenate(planes + [jnp.zeros_like(planes[0])] * (-n_exp % 8), axis=0)
    wanted = jnp.where(dot_nt(planes.astype(BF16), parents) > 0.5, 1.0, 0.0)
    code_z = code_of(wanted, in_block)
    code_z_back = code_of(planes, in_block)
    for s in range(n_exp):
        plane = lax.rem(my_exp + s, n_exp)
        pack[s * cap_z : (s + 1) * cap_z, :] = slots_of(one_row(code_z[:, :rows], plane), cap_z)
        unpack[s * cap_z_back : (s + 1) * cap_z_back, :] = slots_of(
            one_row(code_z_back[:, :rows], plane), cap_z_back
        )

    turn = lax.div(flat_iota((1, group), 1), rows).astype(jnp.float32)

    def packed(code, slots):
        code = one_row(code, my_exp)
        held = (code > 0.5) & (code < slots + 0.5)
        return slots_of(jnp.where(held, turn * slots + code, 0.0), n_exp * slots)

    held = packed(code_z, cap_z)
    held_back = packed(code_z_back, cap_z_back)

    visits = []
    for pair in range(n_pair):
        for z in range(n_exp):
            first = float(2 * pair * n_exp + z)
            visits.append(any_hit((named == first) | (named == first + n_exp)))
    visits = jnp.concatenate(visits + [jnp.zeros_like(visits[0])] * (-len(visits) % 8), axis=0)
    needs = jnp.where(dot_nt(visits.astype(BF16), parents) > 0.5, 1.0, 0.0)
    code = code_of(needs, in_group)
    code_back = code_of(visits, in_group)
    for k in range(n_pair):
        pair = lax.div(lax.bitwise_xor(my_rep, 2 * k), 2)
        row = pair * n_exp + my_exp
        chosen = slots_of(one_row(code, row), cap)
        select[k * cap : (k + 1) * cap, :] = dot_nt(chosen, held).astype(BF16)
        chosen = slots_of(one_row(code_back, row), cap_back)
        expand[:, k * cap_back : (k + 1) * cap_back] = dot_nt(held_back, chosen).astype(BF16)

    over = jnp.maximum(jnp.max(code_z) - cap_z, jnp.max(code_z_back) - cap_z_back)
    over = jnp.maximum(over, jnp.max(code) - cap)
    over = jnp.maximum(over, jnp.max(code_back) - cap_back)
    facts[FITS_ROW : FITS_ROW + 1, :] = jnp.where(over > 0.5, 0.0, 1.0) * jnp.ones((1, group))


def pair_plan(sizes, place, *refs):
    n_rep, n_exp, rows, cap, cap_back, cap_z, cap_z_back = sizes
    group = rows * n_exp
    n_pair = n_rep // 2
    high, low = refs[n_pair:]
    my_rep = place[0]
    my_exp = place[1]
    in_group = before_table(group, group)
    own = my_rep * n_exp + my_exp
    other = lax.bitwise_xor(my_rep, 1) * n_exp + my_exp
    for k in range(n_pair):
        named = refs[k][0:8, :].astype(jnp.int32)
        weights = refs[k][WEIGHT_ROW : WEIGHT_ROW + 8, :]
        parents = parent_table(refs[k][PARENT_ROW : PARENT_ROW + 1, :], group)
        visit = any_hit((named == own) | (named == other)) * jnp.ones((8, 1), jnp.float32)
        needs = jnp.where(dot_nt(visit.astype(BF16), parents) > 0.5, 1.0, 0.0)
        code = code_of(needs, in_group)[0:1, :]
        code_back = code_of(visit, in_group)[0:1, :]
        source = dot(slots_of(code, cap), parents).astype(BF16)
        target = slots_of(code_back, cap_back).astype(jnp.float32)
        for at, expert in enumerate((own, other)):
            weight = jnp.sum(jnp.where(named == expert, weights, 0.0), axis=0, keepdims=True)
            weight_high = weight.astype(BF16).astype(jnp.float32)
            for out, value in ((high, weight_high), (low, weight - weight_high)):
                table = dot_nt((target * value).astype(BF16), source).astype(BF16)
                out[k * cap_back : (k + 1) * cap_back, at * cap : (at + 1) * cap] = table


def plan_call(body, shapes, place, *tables):
    whole = pl.BlockSpec(memory_space=pltpu.VMEM)
    return pl.pallas_call(
        body,
        out_shape=[jax.ShapeDtypeStruct(shape, kind) for shape, kind in shapes],
        in_specs=[pl.BlockSpec(memory_space=pltpu.SMEM)] + [whole] * len(tables),
        out_specs=[whole] * len(shapes),
        compiler_params=pltpu.CompilerParams(vmem_limit_bytes=48 * 1024 * 1024),
    )(place, *tables)


def column_parts(width, parts):
    unit = width // sum(parts)
    ends = [unit * sum(parts[: i + 1]) for i in range(len(parts))]
    return [slice(end - unit * part, end) for part, end in zip(parts, ends)]


def shards(hidden, parents, routes, gates, counts, norm_gain, w_gate, w_up, w_down):
    rows, width = hidden.shape
    top = routes.shape[1]
    n_rep = lax.axis_size("rep")
    n_exp = lax.axis_size("exp")
    n_pair = n_rep // 2
    group = rows * n_exp
    my_rep = lax.axis_index("rep")
    my_exp = lax.axis_index("exp")
    most = (rows * top // (n_rep * n_exp) + 2) * n_exp
    cap = round_up(most + most // 8, 16)
    cap_back = round_up(most + most // 4, 16)
    cap_z = rows // 2
    cap_z_back = rows // 2
    sizes = (n_rep, n_exp, rows, cap, cap_back, cap_z, cap_z_back)
    place = jnp.stack([my_rep, my_exp]).astype(jnp.int32)

    value = hidden.astype(jnp.float32)
    scale = lax.rsqrt(jnp.mean(value * value, axis=1, keepdims=True) + 1e-06)
    normed = (value * scale * norm_gain).astype(BF16)

    def one_pass(level, index):
        given = jnp.stack([counts[0], level, index])
        (own,) = plan_call(
            own_facts,
            [((FACTS, rows), jnp.float32)],
            given,
            routes.T,
            gates.T,
            parents[None, :],
        )
        blocks = [ring(own, "exp", n_exp, s) for s in range(n_exp)]
        facts, pack, unpack, select, expand = plan_call(
            functools.partial(group_plan, sizes),
            [
                ((FACTS, group), jnp.float32),
                ((n_exp * cap_z, rows), BF16),
                ((n_exp * cap_z_back, rows), BF16),
                ((n_pair * cap, n_exp * cap_z), BF16),
                ((n_exp * cap_z_back, n_pair * cap_back), BF16),
            ],
            place,
            *blocks,
        )
        def packed(cols, normed):
            return [
                dot(pack[s * cap_z : (s + 1) * cap_z], normed[:, cols]).astype(BF16)
                for s in range(n_exp)
            ]

        def along_exp(sent):
            return [ring(sent[s], "exp", n_exp, s) for s in range(n_exp)]

        def to_pairs(held):
            held = jnp.concatenate(held, axis=0)
            sent = [dot(select[k * cap : (k + 1) * cap], held).astype(BF16) for k in range(n_pair)]
            return [flip(sent[k], n_rep, 2 * k) for k in range(n_pair)]

        in_cols = column_parts(width, IN_PARTS)
        last = len(in_cols) - 1
        shared = normed
        sent, facts = lax.optimization_barrier((packed(in_cols[0], shared), facts))
        held = along_exp(sent)
        served = [flip(facts, n_rep, 2 * k) for k in range(n_pair)]
        high, low = plan_call(
            functools.partial(pair_plan, sizes),
            [((n_pair * cap_back, 2 * cap), BF16)] * 2,
            place,
            *served,
        )
        fits = functools.reduce(jnp.minimum, [other[PARENT_ROW:, : 128] for other in served])
        high, shared = lax.optimization_barrier((high, shared))
        ahead = along_exp(packed(in_cols[1], shared))
        moved = to_pairs(held)
        held = ahead
        fits = jnp.minimum(fits, flip(fits, n_rep, 1))
        sums = (0.0, 0.0, 0.0, 0.0)
        for part, cols in enumerate(in_cols):
            if part < last:
                held, shared, sums, high, low, fits = lax.optimization_barrier(
                    (held, shared, sums, high, low, fits)
                )
                after = to_pairs(held)
                if part + 1 < last:
                    held = along_exp(packed(in_cols[part + 2], shared))
            moved, sums = lax.optimization_barrier((moved, sums))
            arrived = jnp.concatenate(moved, axis=0)
            swapped = flip(arrived, n_rep, 1)
            sums = (
                sums[0] + dot(arrived, w_gate[0, cols]),
                sums[1] + dot(arrived, w_up[0, cols]),
                sums[2] + dot(swapped, w_gate[0, cols]),
                sums[3] + dot(swapped, w_up[0, cols]),
            )
            moved = after
        acts = [(jax.nn.silu(sums[i]) * sums[i + 1]).astype(BF16) for i in (0, 2)]

        def weighted(cols, acts):
            given = flip(dot(acts[1], w_down[0, :, cols]).astype(BF16), n_rep, 1)
            own = dot(acts[0], w_down[0, :, cols]).astype(BF16)
            totals = []
            for k in range(n_pair):
                at = slice(k * cap, (k + 1) * cap)
                both = jnp.concatenate([own[at], given[at]], axis=0)
                to = slice(k * cap_back, (k + 1) * cap_back)
                totals.append((dot(high[to], both) + dot(low[to], both)).astype(BF16))
            return totals

        out_cols = column_parts(width, OUT_PARTS)
        last = len(out_cols) - 1
        parts = []
        totals, acts = lax.optimization_barrier((weighted(out_cols[0], acts), acts))
        moved = [flip(totals[k], n_rep, 2 * k) for k in range(n_pair)]
        totals, acts = lax.optimization_barrier((weighted(out_cols[1], acts), acts))
        for part in range(last + 1):
            if part < last:
                after = [flip(totals[k], n_rep, 2 * k) for k in range(n_pair)]
            moved, acts, parts = lax.optimization_barrier((moved, acts, parts))
            partial = dot(expand, jnp.concatenate(moved, axis=0)).astype(BF16)
            parts = parts + [
                [
                    ring(partial[s * cap_z_back : (s + 1) * cap_z_back], "exp", n_exp, -s)
                    for s in range(n_exp)
                ]
            ]
            if part + 1 < last:
                totals = weighted(out_cols[part + 2], acts)
            moved = after
        mixed = [dot_tn(unpack, jnp.concatenate(part, axis=0)).astype(BF16) for part in parts]
        return jnp.concatenate(mixed, axis=1), fits[FITS_ROW - PARENT_ROW, 0] > 0.5

    def unfinished(state):
        return state[1] < state[0]

    def go_on(state):
        level, index, total = state
        mixed, fit = one_pass(level, index)
        total = jnp.where(index == 0, mixed, total + mixed)
        return jnp.where(fit, level, 2 * level), jnp.where(fit, index + 1, 0), total

    start = (jnp.int32(1), jnp.int32(0), jnp.zeros((rows, width), BF16))
    return lax.while_loop(unfinished, go_on, start)[2]


def solution(mesh):
    placed = (
        P(("rep", "exp"), None),
        P(("rep", "exp")),
        P(("rep", "exp"), None),
        P(("rep", "exp"), None),
        P(("rep", "exp")),
        P(),
        P(("rep", "exp"), None, None),
        P(("rep", "exp"), None, None),
        P(("rep", "exp"), None, None),
    )
    return jax.shard_map(
        shards, mesh=mesh, in_specs=placed, out_specs=P(("rep", "exp"), None), check_vma=False
    )
```

```python
import functools

import jax
import jax.numpy as jnp
from jax import lax
from jax.experimental import pallas as pl
from jax.experimental.pallas import tpu as pltpu
from jax.sharding import PartitionSpec as P

IN_PARTS = (4, 7, 5)
OUT_PARTS = (4, 7, 5)
FACTS = 24
WEIGHT_ROW = 8
PARENT_ROW = 16
FITS_ROW = 17
BF16 = jnp.bfloat16


def dot(a, b):
    return jnp.dot(a, b, preferred_element_type=jnp.float32)


def dot_nt(a, b):
    return lax.dot_general(a, b, (((1,), (1,)), ((), ())), preferred_element_type=jnp.float32)


def dot_tn(a, b):
    return lax.dot_general(a, b, (((0,), (0,)), ((), ())), preferred_element_type=jnp.float32)


def round_up(value, unit):
    return -(-value // unit) * unit


def ring(value, axis, size, shift):
    if shift % size == 0:
        return value
    return lax.ppermute(value, axis, [(i, (i + shift) % size) for i in range(size)])


def flip(value, size, mask):
    if mask == 0:
        return value
    return lax.ppermute(value, "rep", [(i, i ^ mask) for i in range(size)])


def flat_iota(shape, dim):
    return lax.broadcasted_iota(jnp.int32, shape, dim)


def ones_where(condition):
    return jnp.where(condition, 1.0, 0.0).astype(BF16)


def any_hit(hits):
    return jnp.max(jnp.where(hits, 1.0, 0.0), axis=0, keepdims=True)


def parent_table(parent, group):
    return ones_where(flat_iota((group, group), 0) == parent.astype(jnp.int32))


def before_table(group, block):
    a = flat_iota((group, group), 0)
    b = flat_iota((group, group), 1)
    if block == group:
        return ones_where(a < b)
    low = b - lax.rem(b, block)
    return ones_where((a < b) & (a >= low))


def code_of(used, before):
    rank = dot(used.astype(BF16), before)
    return jnp.where(used > 0.5, rank + 1.0, 0.0)


def one_row(table, row):
    chosen = flat_iota(table.shape, 0) == row
    return jnp.sum(jnp.where(chosen, table, 0.0), axis=0, keepdims=True)


def slots_of(code, slots):
    return ones_where(flat_iota((slots, code.shape[1]), 0) + 1 == code.astype(jnp.int32))


def own_facts(given, routes, gates, parents, facts):
    column = flat_iota((1, routes.shape[1]), 1)
    live = (column < given[0]) & (lax.rem(column, given[1]) == given[2])
    scores = gates[...]
    weights = scores / jnp.sum(scores, axis=0, keepdims=True) * jnp.where(live, 1.0, 0.0)
    facts[...] = jnp.zeros_like(facts)
    facts[0:8, :] = jnp.where(live, routes[...], -1).astype(jnp.float32)
    facts[WEIGHT_ROW : WEIGHT_ROW + 8, :] = weights
    facts[PARENT_ROW : PARENT_ROW + 1, :] = parents[...].astype(jnp.float32)


def group_plan(sizes, place, *refs):
    n_rep, n_exp, rows, cap, cap_back, cap_z, cap_z_back = sizes
    blocks = refs[:n_exp]
    facts, pack, unpack, select, expand = refs[n_exp:]
    group = rows * n_exp
    n_pair = n_rep // 2
    my_rep = place[0]
    my_exp = place[1]
    for s in range(n_exp):
        facts[:, s * rows : (s + 1) * rows] = blocks[s][...]
    named = facts[0:8, :]
    parent = facts[PARENT_ROW : PARENT_ROW + 1, :].astype(jnp.int32)
    block = lax.div(parent, rows)
    parent = parent + (lax.rem(my_exp - block + n_exp, n_exp) - block) * rows
    facts[PARENT_ROW : PARENT_ROW + 1, :] = parent.astype(jnp.float32)
    parents = parent_table(parent, group)
    in_block = before_table(group, rows)
    in_group = before_table(group, group)

    lane = named - jnp.floor((named + 0.5) / n_exp) * n_exp
    planes = [any_hit((lane == float(z)) & (named >= 0.0)) for z in range(n_exp)]
    planes = jnp.concatenate(planes + [jnp.zeros_like(planes[0])] * (-n_exp % 8), axis=0)
    wanted = jnp.where(dot_nt(planes.astype(BF16), parents) > 0.5, 1.0, 0.0)
    code_z = code_of(wanted, in_block)
    code_z_back = code_of(planes, in_block)
    for s in range(n_exp):
        plane = lax.rem(my_exp + s, n_exp)
        pack[s * cap_z : (s + 1) * cap_z, :] = slots_of(one_row(code_z[:, :rows], plane), cap_z)
        unpack[s * cap_z_back : (s + 1) * cap_z_back, :] = slots_of(
            one_row(code_z_back[:, :rows], plane), cap_z_back
        )

    turn = lax.div(flat_iota((1, group), 1), rows).astype(jnp.float32)

    def packed(code, slots):
        code = one_row(code, my_exp)
        held = (code > 0.5) & (code < slots + 0.5)
        return slots_of(jnp.where(held, turn * slots + code, 0.0), n_exp * slots)

    held = packed(code_z, cap_z)
    held_back = packed(code_z_back, cap_z_back)

    visits = []
    for pair in range(n_pair):
        for z in range(n_exp):
            first = float(2 * pair * n_exp + z)
            visits.append(any_hit((named == first) | (named == first + n_exp)))
    visits = jnp.concatenate(visits + [jnp.zeros_like(visits[0])] * (-len(visits) % 8), axis=0)
    needs = jnp.where(dot_nt(visits.astype(BF16), parents) > 0.5, 1.0, 0.0)
    code = code_of(needs, in_group)
    code_back = code_of(visits, in_group)
    for k in range(n_pair):
        pair = lax.div(lax.bitwise_xor(my_rep, 2 * k), 2)
        row = pair * n_exp + my_exp
        chosen = slots_of(one_row(code, row), cap)
        select[k * cap : (k + 1) * cap, :] = dot_nt(chosen, held).astype(BF16)
        chosen = slots_of(one_row(code_back, row), cap_back)
        expand[:, k * cap_back : (k + 1) * cap_back] = dot_nt(held_back, chosen).astype(BF16)

    over = jnp.maximum(jnp.max(code_z) - cap_z, jnp.max(code_z_back) - cap_z_back)
    over = jnp.maximum(over, jnp.max(code) - cap)
    over = jnp.maximum(over, jnp.max(code_back) - cap_back)
    facts[FITS_ROW : FITS_ROW + 1, :] = jnp.where(over > 0.5, 0.0, 1.0) * jnp.ones((1, group))


def pair_plan(sizes, place, *refs):
    n_rep, n_exp, rows, cap, cap_back, cap_z, cap_z_back = sizes
    group = rows * n_exp
    n_pair = n_rep // 2
    high, low = refs[n_pair:]
    my_rep = place[0]
    my_exp = place[1]
    in_group = before_table(group, group)
    own = my_rep * n_exp + my_exp
    other = lax.bitwise_xor(my_rep, 1) * n_exp + my_exp
    for k in range(n_pair):
        named = refs[k][0:8, :].astype(jnp.int32)
        weights = refs[k][WEIGHT_ROW : WEIGHT_ROW + 8, :]
        parents = parent_table(refs[k][PARENT_ROW : PARENT_ROW + 1, :], group)
        visit = any_hit((named == own) | (named == other)) * jnp.ones((8, 1), jnp.float32)
        needs = jnp.where(dot_nt(visit.astype(BF16), parents) > 0.5, 1.0, 0.0)
        code = code_of(needs, in_group)[0:1, :]
        code_back = code_of(visit, in_group)[0:1, :]
        source = dot(slots_of(code, cap), parents).astype(BF16)
        target = slots_of(code_back, cap_back).astype(jnp.float32)
        for at, expert in enumerate((own, other)):
            weight = jnp.sum(jnp.where(named == expert, weights, 0.0), axis=0, keepdims=True)
            weight_high = weight.astype(BF16).astype(jnp.float32)
            for out, value in ((high, weight_high), (low, weight - weight_high)):
                table = dot_nt((target * value).astype(BF16), source).astype(BF16)
                out[k, :, at * cap : (at + 1) * cap] = table


def plan_call(body, shapes, place, *tables):
    whole = pl.BlockSpec(memory_space=pltpu.VMEM)
    return pl.pallas_call(
        body,
        out_shape=[jax.ShapeDtypeStruct(shape, kind) for shape, kind in shapes],
        in_specs=[pl.BlockSpec(memory_space=pltpu.SMEM)] + [whole] * len(tables),
        out_specs=[whole] * len(shapes),
        compiler_params=pltpu.CompilerParams(vmem_limit_bytes=48 * 1024 * 1024),
    )(place, *tables)


def column_parts(width, parts):
    unit = width // sum(parts)
    ends = [unit * sum(parts[: i + 1]) for i in range(len(parts))]
    return [slice(end - unit * part, end) for part, end in zip(parts, ends)]


def shards(hidden, parents, routes, gates, counts, norm_gain, w_gate, w_up, w_down):
    rows, width = hidden.shape
    top = routes.shape[1]
    n_rep = lax.axis_size("rep")
    n_exp = lax.axis_size("exp")
    n_pair = n_rep // 2
    group = rows * n_exp
    my_rep = lax.axis_index("rep")
    my_exp = lax.axis_index("exp")
    most = (rows * top // (n_rep * n_exp) + 2) * n_exp
    cap = round_up(most + most // 8, 16)
    cap_back = round_up(most + most // 4, 16)
    cap_z = rows // 2
    cap_z_back = rows // 2
    sizes = (n_rep, n_exp, rows, cap, cap_back, cap_z, cap_z_back)
    place = jnp.stack([my_rep, my_exp]).astype(jnp.int32)

    def one_pass(level, index):
        given = jnp.stack([counts[0], level, index])
        (own,) = plan_call(
            own_facts,
            [((FACTS, rows), jnp.float32)],
            given,
            routes.T,
            gates.T,
            parents[None, :],
        )
        own, rows_in = lax.optimization_barrier((own, hidden))
        blocks = [ring(own, "exp", n_exp, s) for s in range(n_exp)]
        value = rows_in.astype(jnp.float32)
        scale = lax.rsqrt(jnp.mean(value * value, axis=1, keepdims=True) + 1e-06)
        normed = (value * scale * norm_gain).astype(BF16)
        facts, pack, unpack, select, expand = plan_call(
            functools.partial(group_plan, sizes),
            [
                ((FACTS, group), jnp.float32),
                ((n_exp * cap_z, rows), BF16),
                ((n_exp * cap_z_back, rows), BF16),
                ((n_pair * cap, n_exp * cap_z), BF16),
                ((n_exp * cap_z_back, n_pair * cap_back), BF16),
            ],
            place,
            *blocks,
        )
        def packed(cols, normed):
            return [
                dot(pack[s * cap_z : (s + 1) * cap_z], normed[:, cols]).astype(BF16)
                for s in range(n_exp)
            ]

        def along_exp(sent):
            return [ring(sent[s], "exp", n_exp, s) for s in range(n_exp)]

        def to_pairs(held):
            held = jnp.concatenate(held, axis=0)
            sent = [dot(select[k * cap : (k + 1) * cap], held).astype(BF16) for k in range(n_pair)]
            return [flip(sent[k], n_rep, 2 * k) for k in range(n_pair)]

        in_cols = column_parts(width, IN_PARTS)
        last = len(in_cols) - 1
        shared = normed
        sent, facts = lax.optimization_barrier((packed(in_cols[0], shared), facts))
        held = along_exp(sent)
        served = [flip(facts, n_rep, 2 * k) for k in range(n_pair)]
        high, low = plan_call(
            functools.partial(pair_plan, sizes),
            [((n_pair, cap_back, 2 * cap), BF16)] * 2,
            place,
            *served,
        )
        fits = functools.reduce(jnp.minimum, [other[PARENT_ROW:, : 128] for other in served])
        high, shared = lax.optimization_barrier((high, shared))
        ahead = along_exp(packed(in_cols[1], shared))
        moved = to_pairs(held)
        held = ahead
        fits = jnp.minimum(fits, flip(fits, n_rep, 1))
        sums = (0.0, 0.0, 0.0, 0.0)
        for part, cols in enumerate(in_cols):
            if part < last:
                held, shared, sums, high, low, fits = lax.optimization_barrier(
                    (held, shared, sums, high, low, fits)
                )
                after = to_pairs(held)
                if part + 1 < last:
                    held = along_exp(packed(in_cols[part + 2], shared))
            moved, sums = lax.optimization_barrier((moved, sums))
            arrived = jnp.concatenate(moved, axis=0)
            swapped = flip(arrived, n_rep, 1)
            sums = (
                sums[0] + dot(arrived, w_gate[0, cols]),
                sums[1] + dot(arrived, w_up[0, cols]),
                sums[2] + dot(swapped, w_gate[0, cols]),
                sums[3] + dot(swapped, w_up[0, cols]),
            )
            moved = after
        acts = [(jax.nn.silu(sums[i]) * sums[i + 1]).astype(BF16) for i in (0, 2)]

        def weighted(cols, acts):
            given = flip(dot(acts[1], w_down[0, :, cols]).astype(BF16), n_rep, 1)
            own = dot(acts[0], w_down[0, :, cols]).astype(BF16)
            both = jnp.concatenate(
                [own.reshape(n_pair, cap, -1), given.reshape(n_pair, cap, -1)], axis=1
            )
            total = jnp.einsum("krs,ksd->krd", high, both, preferred_element_type=jnp.float32)
            total += jnp.einsum("krs,ksd->krd", low, both, preferred_element_type=jnp.float32)
            totals = total.astype(BF16)
            return totals

        out_cols = column_parts(width, OUT_PARTS)
        last = len(out_cols) - 1
        parts = []
        totals, acts = lax.optimization_barrier((weighted(out_cols[0], acts), acts))
        moved = [flip(totals[k], n_rep, 2 * k) for k in range(n_pair)]
        totals, acts = lax.optimization_barrier((weighted(out_cols[1], acts), acts))
        for part in range(last + 1):
            moved, totals, acts, parts = lax.optimization_barrier((moved, totals, acts, parts))
            if part < last:
                after = [flip(totals[k], n_rep, 2 * k) for k in range(n_pair)]
            partial = dot(expand, jnp.concatenate(moved, axis=0)).astype(BF16)
            parts = parts + [
                [
                    ring(partial[s * cap_z_back : (s + 1) * cap_z_back], "exp", n_exp, -s)
                    for s in range(n_exp)
                ]
            ]
            if part + 1 < last:
                totals = weighted(out_cols[part + 2], acts)
            moved = after
        mixed = [dot_tn(unpack, jnp.concatenate(part, axis=0)).astype(BF16) for part in parts]
        return jnp.concatenate(mixed, axis=1), fits[FITS_ROW - PARENT_ROW, 0] > 0.5

    def unfinished(state):
        return state[1] < state[0]

    def go_on(state):
        level, index, total = state
        mixed, fit = one_pass(level, index)
        total = jnp.where(index == 0, mixed, total + mixed)
        return jnp.where(fit, level, 2 * level), jnp.where(fit, index + 1, 0), total

    start = (jnp.int32(1), jnp.int32(0), jnp.zeros((rows, width), BF16))
    return lax.while_loop(unfinished, go_on, start)[2]


def solution(mesh):
    placed = (
        P(("rep", "exp"), None),
        P(("rep", "exp")),
        P(("rep", "exp"), None),
        P(("rep", "exp"), None),
        P(("rep", "exp")),
        P(),
        P(("rep", "exp"), None, None),
        P(("rep", "exp"), None, None),
        P(("rep", "exp"), None, None),
    )
    return jax.shard_map(
        shards, mesh=mesh, in_specs=placed, out_specs=P(("rep", "exp"), None), check_vma=False
    )
```

```python
import functools

import jax
import jax.numpy as jnp
from jax import lax
from jax.experimental import pallas as pl
from jax.experimental.pallas import tpu as pltpu
from jax.sharding import PartitionSpec as P

IN_PARTS = (4, 7, 5)
OUT_PARTS = (4, 7, 5)
FACTS = 24
WEIGHT_ROW = 8
PARENT_ROW = 16
FITS_ROW = 17
BF16 = jnp.bfloat16


def dot(a, b):
    return jnp.dot(a, b, preferred_element_type=jnp.float32)


def dot_nt(a, b):
    return lax.dot_general(a, b, (((1,), (1,)), ((), ())), preferred_element_type=jnp.float32)


def dot_tn(a, b):
    return lax.dot_general(a, b, (((0,), (0,)), ((), ())), preferred_element_type=jnp.float32)


def round_up(value, unit):
    return -(-value // unit) * unit


def ring(value, axis, size, shift):
    if shift % size == 0:
        return value
    return lax.ppermute(value, axis, [(i, (i + shift) % size) for i in range(size)])


def flip(value, size, mask):
    if mask == 0:
        return value
    return lax.ppermute(value, "rep", [(i, i ^ mask) for i in range(size)])


def flat_iota(shape, dim):
    return lax.broadcasted_iota(jnp.int32, shape, dim)


def ones_where(condition):
    return jnp.where(condition, 1.0, 0.0).astype(BF16)


def any_hit(hits):
    return jnp.max(jnp.where(hits, 1.0, 0.0), axis=0, keepdims=True)


def parent_table(parent, group):
    return ones_where(flat_iota((group, group), 0) == parent.astype(jnp.int32))


def before_table(group, block):
    a = flat_iota((group, group), 0)
    b = flat_iota((group, group), 1)
    if block == group:
        return ones_where(a < b)
    low = b - lax.rem(b, block)
    return ones_where((a < b) & (a >= low))


def code_of(used, before):
    rank = dot(used.astype(BF16), before)
    return jnp.where(used > 0.5, rank + 1.0, 0.0)


def one_row(table, row):
    chosen = flat_iota(table.shape, 0) == row
    return jnp.sum(jnp.where(chosen, table, 0.0), axis=0, keepdims=True)


def slots_of(code, slots):
    return ones_where(flat_iota((slots, code.shape[1]), 0) + 1 == code.astype(jnp.int32))


def own_facts(given, routes, gates, parents, facts):
    column = flat_iota((1, routes.shape[1]), 1)
    live = (column < given[0]) & (lax.rem(column, given[1]) == given[2])
    scores = gates[...]
    weights = scores / jnp.sum(scores, axis=0, keepdims=True) * jnp.where(live, 1.0, 0.0)
    facts[...] = jnp.zeros_like(facts)
    facts[0:8, :] = jnp.where(live, routes[...], -1).astype(jnp.float32)
    facts[WEIGHT_ROW : WEIGHT_ROW + 8, :] = weights
    facts[PARENT_ROW : PARENT_ROW + 1, :] = parents[...].astype(jnp.float32)


def group_plan(sizes, place, *refs):
    n_rep, n_exp, rows, cap, cap_back, cap_z, cap_z_back = sizes
    blocks = refs[:n_exp]
    facts, pack, unpack, select, expand = refs[n_exp:]
    group = rows * n_exp
    n_pair = n_rep // 2
    my_rep = place[0]
    my_exp = place[1]
    for s in range(n_exp):
        facts[:, s * rows : (s + 1) * rows] = blocks[s][...]
    named = facts[0:8, :]
    parent = facts[PARENT_ROW : PARENT_ROW + 1, :].astype(jnp.int32)
    block = lax.div(parent, rows)
    parent = parent + (lax.rem(my_exp - block + n_exp, n_exp) - block) * rows
    facts[PARENT_ROW : PARENT_ROW + 1, :] = parent.astype(jnp.float32)
    parents = parent_table(parent, group)
    in_block = before_table(group, rows)
    in_group = before_table(group, group)

    lane = named - jnp.floor((named + 0.5) / n_exp) * n_exp
    planes = [any_hit((lane == float(z)) & (named >= 0.0)) for z in range(n_exp)]
    planes = jnp.concatenate(planes + [jnp.zeros_like(planes[0])] * (-n_exp % 8), axis=0)
    wanted = jnp.where(dot_nt(planes.astype(BF16), parents) > 0.5, 1.0, 0.0)
    code_z = code_of(wanted, in_block)
    code_z_back = code_of(planes, in_block)
    for s in range(n_exp):
        plane = lax.rem(my_exp + s, n_exp)
        pack[s * cap_z : (s + 1) * cap_z, :] = slots_of(one_row(code_z[:, :rows], plane), cap_z)
        unpack[s * cap_z_back : (s + 1) * cap_z_back, :] = slots_of(
            one_row(code_z_back[:, :rows], plane), cap_z_back
        )

    turn = lax.div(flat_iota((1, group), 1), rows).astype(jnp.float32)

    def packed(code, slots):
        code = one_row(code, my_exp)
        held = (code > 0.5) & (code < slots + 0.5)
        return slots_of(jnp.where(held, turn * slots + code, 0.0), n_exp * slots)

    held = packed(code_z, cap_z)
    held_back = packed(code_z_back, cap_z_back)

    visits = []
    for pair in range(n_pair):
        for z in range(n_exp):
            first = float(2 * pair * n_exp + z)
            visits.append(any_hit((named == first) | (named == first + n_exp)))
    visits = jnp.concatenate(visits + [jnp.zeros_like(visits[0])] * (-len(visits) % 8), axis=0)
    needs = jnp.where(dot_nt(visits.astype(BF16), parents) > 0.5, 1.0, 0.0)
    code = code_of(needs, in_group)
    code_back = code_of(visits, in_group)
    for k in range(n_pair):
        pair = lax.div(lax.bitwise_xor(my_rep, 2 * k), 2)
        row = pair * n_exp + my_exp
        chosen = slots_of(one_row(code, row), cap)
        select[k * cap : (k + 1) * cap, :] = dot_nt(chosen, held).astype(BF16)
        chosen = slots_of(one_row(code_back, row), cap_back)
        expand[:, k * cap_back : (k + 1) * cap_back] = dot_nt(held_back, chosen).astype(BF16)

    over = jnp.maximum(jnp.max(code_z) - cap_z, jnp.max(code_z_back) - cap_z_back)
    over = jnp.maximum(over, jnp.max(code) - cap)
    over = jnp.maximum(over, jnp.max(code_back) - cap_back)
    facts[FITS_ROW : FITS_ROW + 1, :] = jnp.where(over > 0.5, 0.0, 1.0) * jnp.ones((1, group))


def pair_plan(sizes, place, *refs):
    n_rep, n_exp, rows, cap, cap_back, cap_z, cap_z_back = sizes
    group = rows * n_exp
    n_pair = n_rep // 2
    table_out = refs[n_pair]
    my_rep = place[0]
    my_exp = place[1]
    in_group = before_table(group, group)
    own = my_rep * n_exp + my_exp
    other = lax.bitwise_xor(my_rep, 1) * n_exp + my_exp
    for k in range(n_pair):
        named = refs[k][0:8, :].astype(jnp.int32)
        weights = refs[k][WEIGHT_ROW : WEIGHT_ROW + 8, :]
        parents = parent_table(refs[k][PARENT_ROW : PARENT_ROW + 1, :], group)
        visit = any_hit((named == own) | (named == other)) * jnp.ones((8, 1), jnp.float32)
        needs = jnp.where(dot_nt(visit.astype(BF16), parents) > 0.5, 1.0, 0.0)
        code = code_of(needs, in_group)[0:1, :]
        code_back = code_of(visit, in_group)[0:1, :]
        source = dot(slots_of(code, cap), parents).astype(BF16)
        target = slots_of(code_back, cap_back).astype(jnp.float32)
        for at, expert in enumerate((own, other)):
            weight = jnp.sum(jnp.where(named == expert, weights, 0.0), axis=0, keepdims=True)
            table_out[k, :, at * cap : (at + 1) * cap] = dot_nt(
                (target * weight).astype(BF16), source
            ).astype(BF16)


def plan_call(body, shapes, place, *tables):
    whole = pl.BlockSpec(memory_space=pltpu.VMEM)
    return pl.pallas_call(
        body,
        out_shape=[jax.ShapeDtypeStruct(shape, kind) for shape, kind in shapes],
        in_specs=[pl.BlockSpec(memory_space=pltpu.SMEM)] + [whole] * len(tables),
        out_specs=[whole] * len(shapes),
        compiler_params=pltpu.CompilerParams(vmem_limit_bytes=48 * 1024 * 1024),
    )(place, *tables)


def column_parts(width, parts):
    unit = width // sum(parts)
    ends = [unit * sum(parts[: i + 1]) for i in range(len(parts))]
    return [slice(end - unit * part, end) for part, end in zip(parts, ends)]


def shards(hidden, parents, routes, gates, counts, norm_gain, w_gate, w_up, w_down):
    rows, width = hidden.shape
    top = routes.shape[1]
    n_rep = lax.axis_size("rep")
    n_exp = lax.axis_size("exp")
    n_pair = n_rep // 2
    group = rows * n_exp
    my_rep = lax.axis_index("rep")
    my_exp = lax.axis_index("exp")
    most = (rows * top // (n_rep * n_exp) + 2) * n_exp
    cap = round_up(most + most // 8, 16)
    cap_back = round_up(most + most // 4, 16)
    cap_z = rows // 2
    cap_z_back = rows // 2
    sizes = (n_rep, n_exp, rows, cap, cap_back, cap_z, cap_z_back)
    place = jnp.stack([my_rep, my_exp]).astype(jnp.int32)

    def one_pass(level, index):
        given = jnp.stack([counts[0], level, index])
        (own,) = plan_call(
            own_facts,
            [((FACTS, rows), jnp.float32)],
            given,
            routes.T,
            gates.T,
            parents[None, :],
        )
        own, rows_in = lax.optimization_barrier((own, hidden))
        blocks = [ring(own, "exp", n_exp, s) for s in range(n_exp)]
        value = rows_in.astype(jnp.float32)
        scale = lax.rsqrt(jnp.mean(value * value, axis=1, keepdims=True) + 1e-06)
        normed = (value * scale * norm_gain).astype(BF16)
        facts, pack, unpack, select, expand = plan_call(
            functools.partial(group_plan, sizes),
            [
                ((FACTS, group), jnp.float32),
                ((n_exp * cap_z, rows), BF16),
                ((n_exp * cap_z_back, rows), BF16),
                ((n_pair * cap, n_exp * cap_z), BF16),
                ((n_exp * cap_z_back, n_pair * cap_back), BF16),
            ],
            place,
            *blocks,
        )
        def packed(cols, normed):
            return [
                dot(pack[s * cap_z : (s + 1) * cap_z], normed[:, cols]).astype(BF16)
                for s in range(n_exp)
            ]

        def along_exp(sent):
            return [ring(sent[s], "exp", n_exp, s) for s in range(n_exp)]

        def to_pairs(held):
            held = jnp.concatenate(held, axis=0)
            sent = [dot(select[k * cap : (k + 1) * cap], held).astype(BF16) for k in range(n_pair)]
            return [flip(sent[k], n_rep, 2 * k) for k in range(n_pair)]

        in_cols = column_parts(width, IN_PARTS)
        last = len(in_cols) - 1
        shared = normed
        sent, facts = lax.optimization_barrier((packed(in_cols[0], shared), facts))
        held = along_exp(sent)
        served = [flip(facts, n_rep, 2 * k) for k in range(n_pair)]
        (high,) = plan_call(
            functools.partial(pair_plan, sizes),
            [((n_pair, cap_back, 2 * cap), BF16)],
            place,
            *served,
        )
        fits = functools.reduce(jnp.minimum, [other[PARENT_ROW:, : 128] for other in served])
        high, shared = lax.optimization_barrier((high, shared))
        ahead = along_exp(packed(in_cols[1], shared))
        moved = to_pairs(held)
        held = ahead
        fits = jnp.minimum(fits, flip(fits, n_rep, 1))
        sums = (0.0, 0.0, 0.0, 0.0)
        for part, cols in enumerate(in_cols):
            if part < last:
                held, shared, sums, high, fits = lax.optimization_barrier(
                    (held, shared, sums, high, fits)
                )
                after = to_pairs(held)
                if part + 1 < last:
                    held = along_exp(packed(in_cols[part + 2], shared))
            moved, sums = lax.optimization_barrier((moved, sums))
            arrived = jnp.concatenate(moved, axis=0)
            swapped = flip(arrived, n_rep, 1)
            sums = (
                sums[0] + dot(arrived, w_gate[0, cols]),
                sums[1] + dot(arrived, w_up[0, cols]),
                sums[2] + dot(swapped, w_gate[0, cols]),
                sums[3] + dot(swapped, w_up[0, cols]),
            )
            moved = after
        acts = [(jax.nn.silu(sums[i]) * sums[i + 1]).astype(BF16) for i in (0, 2)]

        def weighted(cols, acts):
            given = flip(dot(acts[1], w_down[0, :, cols]).astype(BF16), n_rep, 1)
            own = dot(acts[0], w_down[0, :, cols]).astype(BF16)
            both = jnp.concatenate(
                [own.reshape(n_pair, cap, -1), given.reshape(n_pair, cap, -1)], axis=1
            )
            total = jnp.einsum("krs,ksd->krd", high, both, preferred_element_type=jnp.float32)
            totals = total.astype(BF16)
            return totals

        out_cols = column_parts(width, OUT_PARTS)
        last = len(out_cols) - 1
        parts = []
        totals, acts = lax.optimization_barrier((weighted(out_cols[0], acts), acts))
        moved = [flip(totals[k], n_rep, 2 * k) for k in range(n_pair)]
        totals, acts = lax.optimization_barrier((weighted(out_cols[1], acts), acts))
        for part in range(last + 1):
            moved, totals, acts, parts = lax.optimization_barrier((moved, totals, acts, parts))
            if part < last:
                after = [flip(totals[k], n_rep, 2 * k) for k in range(n_pair)]
            partial = dot(expand, jnp.concatenate(moved, axis=0)).astype(BF16)
            parts = parts + [
                [
                    ring(partial[s * cap_z_back : (s + 1) * cap_z_back], "exp", n_exp, -s)
                    for s in range(n_exp)
                ]
            ]
            if part + 1 < last:
                totals = weighted(out_cols[part + 2], acts)
            moved = after
        mixed = [dot_tn(unpack, jnp.concatenate(part, axis=0)).astype(BF16) for part in parts]
        return jnp.concatenate(mixed, axis=1), fits[FITS_ROW - PARENT_ROW, 0] > 0.5

    def unfinished(state):
        return state[1] < state[0]

    def go_on(state):
        level, index, total = state
        mixed, fit = one_pass(level, index)
        total = jnp.where(index == 0, mixed, total + mixed)
        return jnp.where(fit, level, 2 * level), jnp.where(fit, index + 1, 0), total

    start = (jnp.int32(1), jnp.int32(0), jnp.zeros((rows, width), BF16))
    return lax.while_loop(unfinished, go_on, start)[2]


def solution(mesh):
    placed = (
        P(("rep", "exp"), None),
        P(("rep", "exp")),
        P(("rep", "exp"), None),
        P(("rep", "exp"), None),
        P(("rep", "exp")),
        P(),
        P(("rep", "exp"), None, None),
        P(("rep", "exp"), None, None),
        P(("rep", "exp"), None, None),
    )
    return jax.shard_map(
        shards, mesh=mesh, in_specs=placed, out_specs=P(("rep", "exp"), None), check_vma=False
    )
```
